1024 devices in a mesh: depth: 16 (over y, core), row: 8 (over x, z_hi), col: 8 (over z_lo).
Axes of the slice: x: 4, y: 8, z: 16 (z_hi: 2, z_lo: 8; z = z_hi * 8 + z_lo), core: 2. Of those that a mesh axis runs over, the one named last changes fastest.
Arguments:
- act_values: bfloat16 [2048, 4096], P('depth', 'row'), may hold values from -6 to 6
- activation_scale: float32 [2048, 32], P('depth', 'row'), may hold values from 0.25 to 4
- token_order: int32 [16, 128], P('depth'), may hold values from 0 to 127, each once within a row
- gate_q: bfloat16 [4096, 14336], P('row', 'col'), may hold values from -0.09375 to 0.09375
- gate_scale: float32 [32, 112], P('row', 'col'), may hold values from 0.5 to 2
- up_q: bfloat16 [4096, 14336], P('row', 'col'), may hold values from -0.09375 to 0.09375
- up_scale: float32 [32, 112], P('row', 'col'), may hold values from 0.5 to 2
- cotangent: bfloat16 [2048, 14336], P(('depth', 'row'), 'col'), may hold values from -5 to 5
Outputs:
- grad_act: bfloat16 [2048, 4096], P(('depth', 'col'), 'row')
- grad_gate: bfloat16 [4096, 14336], P('row', ('col', 'depth'))
- grad_up: bfloat16 [4096, 14336], P('row', ('col', 'depth'))
The draws below stay inside these ranges and needn't reach their ends.
Inputs may be any that keep to these rules, and one draw needn't show every extreme that they name: Each row of token_order is a permutation of 0 to 127.
All inputs are finite; a program needn't handle non-finite values.
Results may differ from the reference program's by a relative error of at most 0.033.
Values may be sent and summed in bfloat16 or wider, within the bound.
No kernel may reach another device: no remote copies, remote signals or barrier semaphores. Data moves between devices by JAX's collectives and lax.ppermute only.
A program may use at most 32 MiB of HBM per device.

```python
import math
import jax
import jax.numpy as jnp
from jax import lax

MODEL_WIDTH = 4096
FF = 14336
GROUP = 128
DEPTH_TOKENS = 128
TOKENS = 2048
TOKEN_BLOCK_COUNT = 16
DG = 32
FG = 112


def raised(result, rng, source, target, shards_of, factor):
    def block_of(position):
        return (jnp.arange(result.shape[position]) // (result.shape[position] // shards_of)).reshape((-1,) + (1,) * (result.ndim - 1 - position))

    near = jax.random.permutation(rng, shards_of)[block_of(target)]
    second = (block_of(target) + shards_of // 2) % shards_of
    return jnp.where((block_of(source) == near) | (block_of(source) == second), factor * result, result)


def block_levels(key, shape, shards, low, high):
    factor_of, own = 1.0, jax.random.fold_in(key, 6)
    for axis_at, blocks in shards:
        heights = jnp.exp(jax.random.uniform(jax.random.fold_in(own, axis_at), (blocks,), jnp.float32, low / len(shards), high / len(shards)))
        factor_of = factor_of * jnp.repeat(heights, shape[axis_at] // blocks).reshape([-1 if axis == axis_at else 1 for axis in range(len(shape))])
    return factor_of


def noise(key, shape, deviation, reach, shards=(), kind=jnp.bfloat16):
    entries = deviation * jax.random.normal(key, shape, jnp.float32)
    if shards:
        entries = entries * block_levels(key, shape, shards, -0.22, 0.18)
    return jnp.clip(entries, -reach, reach).astype(kind)


def heavy_noise(key, shape, width, most, split, heavy, kind=jnp.bfloat16):
    values = width * jax.random.normal(key, shape, jnp.float32)
    if split:
        values = values * block_levels(key, shape, split, -0.22, 0.18)
    return jnp.clip(raised(values, jax.random.fold_in(key, 3), *heavy), -most, most).astype(kind)


def setup_inputs(seed: int = 0) -> dict:
    seeds = jax.random.split(jax.random.key(seed), 9)
    return {
        "act_values": noise(seeds[0], (TOKENS, MODEL_WIDTH), 1.0, 6.0, ((0, 16), (1, 8))),
        "activation_scale": jnp.clip(jnp.exp(math.log(4.0) - 2.7725887 * jax.random.uniform(seeds[1], (TOKENS, DG), jnp.float32) ** block_levels(seeds[1], (TOKENS, DG), ((0, 16), (1, 8)), -0.2, 0.2)), 0.25, 4.0),
        "token_order": jax.vmap(lambda own: jax.random.permutation(own, DEPTH_TOKENS))(jax.random.split(seeds[2], TOKEN_BLOCK_COUNT)).reshape((TOKEN_BLOCK_COUNT, DEPTH_TOKENS)).astype(jnp.int32),
        "gate_q": noise(seeds[3], (MODEL_WIDTH, FF), MODEL_WIDTH ** -0.5, 0.09375, ((0, 8), (1, 8))),
        "gate_scale": jnp.clip(jnp.exp(math.log(2.0) - 1.3862944 * jax.random.uniform(seeds[4], (DG, FG), jnp.float32) ** block_levels(seeds[4], (DG, FG), ((0, 8), (1, 8)), -0.2, 0.2)), 0.5, 2.0),
        "up_q": noise(seeds[5], (MODEL_WIDTH, FF), MODEL_WIDTH ** -0.5, 0.09375, ((0, 8), (1, 8))),
        "up_scale": jnp.clip(jnp.exp(math.log(2.0) - 1.3862944 * jax.random.uniform(seeds[6], (DG, FG), jnp.float32) ** block_levels(seeds[6], (DG, FG), ((0, 8), (1, 8)), -0.2, 0.2)), 0.5, 2.0),
        "cotangent": heavy_noise(seeds[7], (TOKENS, FF), 0.2, 5.0, ((0, 128), (1, 8)), (0, 1, 128, 5.5)),
    }


def dequant_weight(values, scales):
    blocks = values.astype(jnp.float32).reshape(DG, GROUP, FG, GROUP) * scales[:, None, :, None]
    return blocks.reshape(MODEL_WIDTH, FF).astype(jnp.bfloat16)


def reference(act_values, activation_scale, token_order, gate_q, gate_scale, up_q, up_scale, cotangent):
    input_tensors = (act_values.astype(jnp.float32).reshape(TOKENS, DG, GROUP) * activation_scale[:, :, None]).reshape(TOKENS, MODEL_WIDTH).astype(jnp.bfloat16)
    one_hot_matrix = (token_order[:, None, :] == jnp.arange(DEPTH_TOKENS, dtype=jnp.int32)[None, :, None]).astype(jnp.float32)
    natural_order = jnp.einsum("omp,opg->omg", one_hot_matrix, input_tensors.reshape(TOKEN_BLOCK_COUNT, DEPTH_TOKENS, MODEL_WIDTH).astype(jnp.float32)).astype(jnp.bfloat16)
    flat_rows = natural_order.reshape(TOKENS, MODEL_WIDTH)
    gate_weight = dequant_weight(gate_q, gate_scale)
    w_up = dequant_weight(up_q, up_scale)
    gate_pre = jnp.dot(flat_rows, gate_weight, preferred_element_type=jnp.float32)
    up_pre = jnp.dot(flat_rows, w_up, preferred_element_type=jnp.float32)
    sigmoid_gate = jax.nn.sigmoid(gate_pre)
    slope_in = cotangent.astype(jnp.float32)
    d_gate = (slope_in * up_pre * sigmoid_gate * (1.0 + gate_pre * (1.0 - sigmoid_gate))).astype(jnp.bfloat16)
    d_up = (slope_in * gate_pre * sigmoid_gate).astype(jnp.bfloat16)
    grad_act = (jnp.dot(d_gate, gate_weight.T, preferred_element_type=jnp.float32)
                + jnp.dot(d_up, w_up.T, preferred_element_type=jnp.float32)).astype(jnp.bfloat16)

    def add_block(totals, block_index):
        first_row = (block_index * DEPTH_TOKENS).astype(jnp.int32)
        tok_rows = lax.dynamic_slice_in_dim(flat_rows, first_row, DEPTH_TOKENS, 0)
        gate_rows = lax.dynamic_slice_in_dim(d_gate, first_row, DEPTH_TOKENS, 0)
        up_rows = lax.dynamic_slice_in_dim(d_up, first_row, DEPTH_TOKENS, 0)
        part_g = lax.dot_general(tok_rows, gate_rows, (((0,), (0,)), ((), ())), preferred_element_type=jnp.float32).astype(jnp.bfloat16)
        part_u = lax.dot_general(tok_rows, up_rows, (((0,), (0,)), ((), ())), preferred_element_type=jnp.float32).astype(jnp.bfloat16)
        part_g, part_u = lax.optimization_barrier((part_g, part_u))
        return (totals[0] + part_g.astype(jnp.float32), totals[1] + part_u.astype(jnp.float32)), None

    zero_sum = jnp.zeros((MODEL_WIDTH, FF), jnp.float32)
    sums, _ = lax.scan(add_block, (zero_sum, zero_sum), jnp.arange(TOKEN_BLOCK_COUNT, dtype=jnp.int32))
    return grad_act, sums[0].astype(jnp.bfloat16), sums[1].astype(jnp.bfloat16)
```

```python
import functools

import jax
import jax.numpy as jnp
from jax import lax
from jax.experimental import pallas as pl
from jax.experimental.pallas import tpu as pltpu
from jax.sharding import Mesh
from jax.sharding import PartitionSpec as P

GROUP = 128
CHUNK = 256
F32 = jnp.float32
BF16 = jnp.bfloat16


def dequant(q_ref, s_ref, first_group):
    rows = []
    for r in range(q_ref.shape[0] // GROUP):
        tiles = []
        for h in range(CHUNK // GROUP):
            tile = q_ref[r * GROUP : (r + 1) * GROUP, h * GROUP : (h + 1) * GROUP].astype(F32)
            tiles.append((tile * s_ref[r, first_group + h]).astype(BF16))
        rows.append(jnp.concatenate(tiles, axis=1))
    return jnp.concatenate(rows, axis=0)


def forward_kernel(gs_ref, us_ref, act_ref, ast_ref, order_ref, gq_ref, uq_ref, pre_ref, nat_ref):
    j = pl.program_id(0)
    tok, feat = act_ref.shape

    @pl.when(j == 0)
    def _():
        one_hot = (
            lax.broadcasted_iota(jnp.int32, (tok, tok), 0)
            == jnp.broadcast_to(order_ref[...], (tok, tok))
        ).astype(F32).astype(BF16)
        parts = []
        for g in range(feat // GROUP):
            scale = jnp.broadcast_to(ast_ref[g : g + 1, :], (tok, tok)).T
            part = act_ref[:, g * GROUP : (g + 1) * GROUP].astype(F32) * scale
            parts.append(part.astype(BF16))
        scaled = jnp.concatenate(parts, axis=1)
        nat_ref[...] = jnp.dot(one_hot, scaled, preferred_element_type=F32).astype(BF16)

    natural = nat_ref[...]
    for t, (q_ref, s_ref) in enumerate(((gq_ref, gs_ref), (uq_ref, us_ref))):
        w = dequant(q_ref, s_ref, j * (CHUNK // GROUP))
        out = jnp.dot(natural, w, preferred_element_type=F32).astype(BF16)
        pre_ref[:, 0, t] = out.reshape(pre_ref.shape[0], pre_ref.shape[3], CHUNK)


def activation_kernel(where_ref, pre_ref, own_ref, other_ref, d_ref, dp_ref, dg_ref, du_ref):
    first = where_ref[1] == 0
    n_chunks = pre_ref.shape[1]
    for j in range(n_chunks):
        cols = slice(j * CHUNK, (j + 1) * CHUNK)
        own, other = own_ref[:, cols].astype(F32), other_ref[:, cols].astype(F32)
        cot = jnp.concatenate(
            [jnp.where(first, own, other), jnp.where(first, other, own)], axis=0
        )
        gate = pre_ref[0, j, 0].astype(F32) + pre_ref[1, j, 0].astype(F32)
        up = pre_ref[0, j, 1].astype(F32) + pre_ref[1, j, 1].astype(F32)
        s = jax.nn.sigmoid(gate)
        d_gate = (cot * up * s * (1.0 + gate * (1.0 - s))).astype(BF16)
        d_up = (cot * gate * s).astype(BF16)
        d_ref[j, 0] = d_gate
        d_ref[j, 1] = d_up
        dg_ref[:, cols] = d_gate.astype(F32)
        du_ref[:, cols] = d_up.astype(F32)
    parts, width = dp_ref.shape[0], dg_ref.shape[1]
    step = width // parts
    for k in range(parts):
        base = (k * step) // GROUP * GROUP
        span = min(2 * GROUP, width - base)
        shift = k * step - base
        for t, src in enumerate((dg_ref, du_ref)):
            window = src[:, base : base + span]
            if shift:
                window = pltpu.roll(window, span - shift, 1)
            dp_ref[k, :, t * GROUP : (t + 1) * GROUP] = window[:, :GROUP].astype(BF16)


def act_grad_kernel(n_x, where_ref, gs_ref, us_ref, *refs):
    d_refs, (gq_ref, uq_ref, out_ref, acc_ref) = refs[:n_x], refs[n_x:]
    j = pl.program_id(0)
    total = None
    for t, (q_ref, s_ref) in enumerate(((gq_ref, gs_ref), (uq_ref, us_ref))):
        w = dequant(q_ref, s_ref, j * (CHUNK // GROUP))
        rows = jnp.concatenate([r[0, t] for r in d_refs], axis=0)
        part = lax.dot_general(rows, w, (((1,), (1,)), ((), ())), preferred_element_type=F32)
        total = part if total is None else total + part

    @pl.when(j == 0)
    def _():
        acc_ref[...] = total

    @pl.when(j > 0)
    def _():
        acc_ref[...] += total

    @pl.when(j == pl.num_programs(0) - 1)
    def _():
        tok = out_ref.shape[1]
        for k in range(n_x):
            at = lax.rem(where_ref[0] - k + n_x, n_x)
            out_ref[pl.ds(at, 1)] = acc_ref[k * tok : (k + 1) * tok, :].astype(BF16)[None]


def weight_grad_kernel(n_x, where_ref, *refs):
    d_refs, (nat_ref, gate_ref, up_ref) = refs[:n_x], refs[n_x:]
    total = None
    for k in range(n_x):
        at = lax.rem(where_ref[0] - k + n_x, n_x)
        rows = d_refs[k][...]
        rows = rows.reshape(rows.shape[0] * rows.shape[1], rows.shape[2])
        nat = nat_ref[:, pl.ds(at, 1)]
        nat = nat.reshape(rows.shape[0], nat.shape[3])
        part = lax.dot_general(rows, nat, (((0,), (0,)), ((), ())), preferred_element_type=F32)
        total = part if total is None else total + part
    width = gate_ref.shape[0]
    gate_ref[...] = total[:width].astype(BF16)
    up_ref[...] = total[GROUP : GROUP + width].astype(BF16)


def params(mib=48):
    return pltpu.CompilerParams(vmem_limit_bytes=mib * 1024 * 1024)


def ring(n, k):
    return [(i, (i + k) % n) for i in range(n)]


def on_device(
    act_values, activation_scale, token_order, gate_q, gate_scale, up_q, up_scale, cotangent
):
    n_x, n_zh = lax.axis_size("x"), lax.axis_size("zh")
    n_depth = lax.axis_size("y") * lax.axis_size("core")
    n_col = lax.axis_size("zl")
    tok, feat = act_values.shape
    hidden = gate_q.shape[1]
    n_chunks = hidden // CHUNK
    rows = tok // n_x
    slice_width = hidden // n_depth
    where = jnp.stack([lax.axis_index("x"), lax.axis_index("zh")]).astype(jnp.int32)
    smem = pl.BlockSpec(memory_space=pltpu.SMEM)
    vmem = pl.BlockSpec(memory_space=pltpu.VMEM)

    cot_other = lax.ppermute(cotangent, "zh", ring(n_zh, 1))

    q_spec = pl.BlockSpec((feat, CHUNK), lambda j: (0, j))
    pre, natural = pl.pallas_call(
        forward_kernel,
        grid=(n_chunks,),
        in_specs=[
            smem,
            smem,
            pl.BlockSpec((tok, feat), lambda j: (0, 0)),
            pl.BlockSpec((feat // GROUP, tok), lambda j: (0, 0)),
            pl.BlockSpec((1, tok), lambda j: (0, 0)),
            q_spec,
            q_spec,
        ],
        out_specs=[
            pl.BlockSpec((n_x, 1, 2, rows, CHUNK), lambda j: (0, j, 0, 0, 0)),
            pl.BlockSpec((tok, feat), lambda j: (0, 0)),
        ],
        out_shape=[
            jax.ShapeDtypeStruct((n_x, n_chunks, 2, rows, CHUNK), BF16),
            jax.ShapeDtypeStruct((tok, feat), BF16),
        ],
        compiler_params=params(),
        name="forward",
    )(gate_scale, up_scale, act_values, activation_scale.T, token_order, gate_q, up_q)

    nat_all = lax.all_gather(natural, ("y", "core"), axis=0, tiled=False)
    nat_all = nat_all.reshape(n_depth, n_x, rows, feat)

    got = lax.all_to_all(pre, "x", 0, 0, tiled=True)
    part = jnp.sum(got.astype(F32), axis=0).astype(BF16)
    both = lax.all_gather(part, "zh", axis=0, tiled=False)

    d, d_split = pl.pallas_call(
        activation_kernel,
        in_specs=[smem, vmem, vmem, vmem],
        out_specs=[vmem, vmem],
        out_shape=[
            jax.ShapeDtypeStruct((n_chunks, 2, rows, CHUNK), BF16),
            jax.ShapeDtypeStruct((n_depth, rows, 2 * GROUP), BF16),
        ],
        scratch_shapes=[pltpu.VMEM((rows, hidden), F32), pltpu.VMEM((rows, hidden), F32)],
        compiler_params=params(),
        name="activation",
    )(where, both, cotangent, cot_other)

    d_x = [d] + [lax.ppermute(d, "x", ring(n_x, k)) for k in range(1, n_x)]
    d_depth = lax.all_to_all(d_split, ("y", "core"), 0, 0, tiled=True)

    d_spec = pl.BlockSpec((1, 2, rows, CHUNK), lambda j: (j, 0, 0, 0))
    act_part = pl.pallas_call(
        functools.partial(act_grad_kernel, n_x),
        grid=(n_chunks,),
        in_specs=[smem, smem, smem] + [d_spec] * n_x + [q_spec, q_spec],
        out_specs=pl.BlockSpec((n_x, rows, feat), lambda j: (0, 0, 0)),
        out_shape=jax.ShapeDtypeStruct((n_x, rows, feat), BF16),
        scratch_shapes=[pltpu.VMEM((tok, feat), F32)],
        compiler_params=params(),
        name="act_grad",
    )(where, gate_scale, up_scale, *d_x, gate_q, up_q)

    d_w = [d_depth] + [lax.ppermute(d_depth, "x", ring(n_x, k)) for k in range(1, n_x)]
    got_act = lax.all_to_all(act_part.reshape(n_col, tok // n_col, feat), "zl", 0, 0, tiled=True)
    grad_act = jnp.sum(got_act.astype(F32), axis=0).astype(BF16)

    gate_t, up_t = pl.pallas_call(
        functools.partial(weight_grad_kernel, n_x),
        in_specs=[smem] + [vmem] * (n_x + 1),
        out_specs=[vmem, vmem],
        out_shape=[jax.ShapeDtypeStruct((slice_width, feat), BF16)] * 2,
        compiler_params=params(),
        name="weight_grad",
    )(where, *d_w, nat_all)
    return grad_act, gate_t.T, up_t.T


def solution(mesh):
    sizes = mesh.shape
    n_zh, n_core = 2, 2
    fine = Mesh(
        mesh.devices.reshape(
            sizes["depth"] // n_core, n_core, sizes["row"] // n_zh, n_zh, sizes["col"]
        ),
        ("y", "core", "x", "zh", "zl"),
    )
    depth, row, col = ("y", "core"), ("x", "zh"), "zl"
    return jax.shard_map(
        on_device,
        mesh=fine,
        in_specs=(
            P(depth, row),
            P(depth, row),
            P(depth, None),
            P(row, col),
            P(row, col),
            P(row, col),
            P(row, col),
            P(depth + row, col),
        ),
        out_specs=(
            P(depth + (col,), row),
            P(row, (col,) + depth),
            P(row, (col,) + depth),
        ),
        check_vma=False,
    )
```

```python
import jax
import jax.numpy as jnp
from jax import lax
from jax.experimental import pallas as pl
from jax.experimental.pallas import tpu as pltpu
from jax.sharding import Mesh
from jax.sharding import PartitionSpec as P

GROUP = 128
CHUNK = 256
F32 = jnp.float32
BF16 = jnp.bfloat16


def dequant(q_ref, s_ref, first_group):
    rows = []
    for r in range(q_ref.shape[0] // GROUP):
        tiles = []
        for h in range(CHUNK // GROUP):
            tile = q_ref[r * GROUP : (r + 1) * GROUP, h * GROUP : (h + 1) * GROUP].astype(F32)
            tiles.append((tile * s_ref[r, first_group + h]).astype(BF16))
        rows.append(jnp.concatenate(tiles, axis=1))
    return jnp.concatenate(rows, axis=0)


def forward_kernel(gs_ref, us_ref, act_ref, ast_ref, order_ref, gq_ref, uq_ref, pre_ref, nat_ref):
    j = pl.program_id(0)
    tok, feat = act_ref.shape

    @pl.when(j == 0)
    def _():
        one_hot = (
            lax.broadcasted_iota(jnp.int32, (tok, tok), 0)
            == jnp.broadcast_to(order_ref[...], (tok, tok))
        ).astype(F32).astype(BF16)
        parts = []
        for g in range(feat // GROUP):
            scale = jnp.broadcast_to(ast_ref[g : g + 1, :], (tok, tok)).T
            part = act_ref[:, g * GROUP : (g + 1) * GROUP].astype(F32) * scale
            parts.append(part.astype(BF16))
        scaled = jnp.concatenate(parts, axis=1)
        nat_ref[...] = jnp.dot(one_hot, scaled, preferred_element_type=F32).astype(BF16)

    natural = nat_ref[...]
    for t, (q_ref, s_ref) in enumerate(((gq_ref, gs_ref), (uq_ref, us_ref))):
        w = dequant(q_ref, s_ref, j * (CHUNK // GROUP))
        out = jnp.dot(natural, w, preferred_element_type=F32).astype(BF16)
        pre_ref[:, 0, t] = out.reshape(pre_ref.shape[0], pre_ref.shape[3], CHUNK)


def reduce_kernel(got_ref, cot_ref, out_ref):
    n_chunks, rows = got_ref.shape[1], got_ref.shape[3]
    for j in range(n_chunks):
        for t in range(2):
            total = got_ref[0, j, t].astype(F32)
            for i in range(1, got_ref.shape[0]):
                total += got_ref[i, j, t].astype(F32)
            out_ref[j, t * rows : (t + 1) * rows] = total.astype(BF16)
        out_ref[j, 2 * rows :] = cot_ref[:, j * CHUNK : (j + 1) * CHUNK]


def activation_kernel(pre_ref, d_ref, dp_ref, dg_ref, du_ref):
    n_zh, n_chunks = pre_ref.shape[0], pre_ref.shape[1]
    rows = dp_ref.shape[1]
    for j in range(n_chunks):
        cols = slice(j * CHUNK, (j + 1) * CHUNK)
        gate, up = (
            sum(pre_ref[i, j, t * rows : (t + 1) * rows].astype(F32) for i in range(n_zh))
            for t in range(2)
        )
        cot = jnp.concatenate([pre_ref[i, j, 2 * rows :] for i in range(n_zh)], axis=0).astype(F32)
        s = jax.nn.sigmoid(gate)
        d_gate = (cot * up * s * (1.0 + gate * (1.0 - s))).astype(BF16)
        d_up = (cot * gate * s).astype(BF16)
        d_ref[j, 0] = d_gate
        d_ref[j, 1] = d_up
        dg_ref[:, cols] = d_gate.astype(F32)
        du_ref[:, cols] = d_up.astype(F32)
    parts, width = dp_ref.shape[0], dg_ref.shape[1]
    step = width // parts
    for k in range(parts):
        base = (k * step) // GROUP * GROUP
        span = min(2 * GROUP, width - base)
        shift = k * step - base
        for t, src in enumerate((dg_ref, du_ref)):
            window = src[:, base : base + span]
            if shift:
                window = pltpu.roll(window, span - shift, 1)
            dp_ref[k, :, t * GROUP : (t + 1) * GROUP] = window[:, :GROUP].astype(BF16)


def act_grad_kernel(gs_ref, us_ref, d_ref, gq_ref, uq_ref, out_ref, acc_ref):
    j = pl.program_id(0)
    total = None
    for t, (q_ref, s_ref) in enumerate(((gq_ref, gs_ref), (uq_ref, us_ref))):
        w = dequant(q_ref, s_ref, j * (CHUNK // GROUP))
        rows = d_ref[:, 0, t].reshape(acc_ref.shape[0], CHUNK)
        part = lax.dot_general(rows, w, (((1,), (1,)), ((), ())), preferred_element_type=F32)
        total = part if total is None else total + part

    @pl.when(j == 0)
    def _():
        acc_ref[...] = total

    @pl.when(j > 0)
    def _():
        acc_ref[...] += total

    @pl.when(j == pl.num_programs(0) - 1)
    def _():
        out_ref[...] = acc_ref[...].astype(BF16)


def finish_kernel(dw_ref, nat_ref, got_ref, gate_ref, up_ref, act_ref, acc_ref):
    k = pl.program_id(0)
    rows = dw_ref[0].reshape(dw_ref.shape[1] * dw_ref.shape[2], dw_ref.shape[3])
    nat = nat_ref[:, 0].reshape(rows.shape[0], nat_ref.shape[3])
    part = lax.dot_general(rows, nat, (((0,), (0,)), ((), ())), preferred_element_type=F32)

    @pl.when(k == 0)
    def _():
        acc_ref[...] = part
        act_ref[...] = sum(got_ref[i].astype(F32) for i in range(got_ref.shape[0])).astype(BF16)

    @pl.when(k > 0)
    def _():
        acc_ref[...] += part

    @pl.when(k == pl.num_programs(0) - 1)
    def _():
        width = gate_ref.shape[0]
        gate_ref[...] = acc_ref[:width].astype(BF16)
        up_ref[...] = acc_ref[GROUP : GROUP + width].astype(BF16)


def params(mib=60):
    return pltpu.CompilerParams(vmem_limit_bytes=mib * 1024 * 1024)


def on_device(
    act_values, activation_scale, token_order, gate_q, gate_scale, up_q, up_scale, cotangent
):
    n_x, n_zh = lax.axis_size("x"), lax.axis_size("zh")
    n_depth = lax.axis_size("y") * lax.axis_size("core")
    n_col = lax.axis_size("zl")
    tok, feat = act_values.shape
    hidden = gate_q.shape[1]
    n_chunks = hidden // CHUNK
    rows = tok // n_x
    slice_width = hidden // n_depth
    smem = pl.BlockSpec(memory_space=pltpu.SMEM)
    vmem = pl.BlockSpec(memory_space=pltpu.VMEM)

    q_spec = pl.BlockSpec((feat, CHUNK), lambda j: (0, j))
    pre, natural = pl.pallas_call(
        forward_kernel,
        grid=(n_chunks,),
        in_specs=[
            smem,
            smem,
            pl.BlockSpec((tok, feat), lambda j: (0, 0)),
            pl.BlockSpec((feat // GROUP, tok), lambda j: (0, 0)),
            pl.BlockSpec((1, tok), lambda j: (0, 0)),
            q_spec,
            q_spec,
        ],
        out_specs=[
            pl.BlockSpec((n_x, 1, 2, rows, CHUNK), lambda j: (0, j, 0, 0, 0)),
            pl.BlockSpec((tok, feat), lambda j: (0, 0)),
        ],
        out_shape=[
            jax.ShapeDtypeStruct((n_x, n_chunks, 2, rows, CHUNK), BF16),
            jax.ShapeDtypeStruct((tok, feat), BF16),
        ],
        compiler_params=params(),
        name="forward",
    )(gate_scale, up_scale, act_values, activation_scale.T, token_order, gate_q, up_q)

    nat_all = lax.all_gather(natural, ("y", "core"), axis=0, tiled=False)
    nat_all = nat_all.reshape(n_depth, n_x, rows, feat)

    got = lax.all_to_all(pre, "x", 0, 0, tiled=True)
    packed = pl.pallas_call(
        reduce_kernel,
        in_specs=[vmem, vmem],
        out_specs=vmem,
        out_shape=jax.ShapeDtypeStruct((n_chunks, 2 * rows + rows // n_zh, CHUNK), BF16),
        compiler_params=params(16),
        name="reduce",
    )(got, cotangent)
    both = lax.all_gather(packed, "zh", axis=0, tiled=False)

    d, d_split = pl.pallas_call(
        activation_kernel,
        in_specs=[vmem],
        out_specs=[vmem, vmem],
        out_shape=[
            jax.ShapeDtypeStruct((n_chunks, 2, rows, CHUNK), BF16),
            jax.ShapeDtypeStruct((n_depth, rows, 2 * GROUP), BF16),
        ],
        scratch_shapes=[pltpu.VMEM((rows, hidden), F32), pltpu.VMEM((rows, hidden), F32)],
        compiler_params=params(16),
        name="activation",
    )(both)

    d_depth = lax.all_to_all(d_split, ("y", "core"), 0, 0, tiled=True)
    d_all = lax.all_gather(d, "x", axis=0, tiled=False)
    d_all, d_depth = lax.optimization_barrier((d_all, d_depth))
    d_copies = jnp.broadcast_to(d_depth[None], (n_x,) + d_depth.shape)
    d_w = lax.all_to_all(d_copies, "x", 0, 0, tiled=True)

    act_part = pl.pallas_call(
        act_grad_kernel,
        grid=(n_chunks,),
        in_specs=[
            smem,
            smem,
            pl.BlockSpec((n_x, 1, 2, rows, CHUNK), lambda j: (0, j, 0, 0, 0)),
            q_spec,
            q_spec,
        ],
        out_specs=pl.BlockSpec((tok, feat), lambda j: (0, 0)),
        out_shape=jax.ShapeDtypeStruct((tok, feat), BF16),
        scratch_shapes=[pltpu.VMEM((tok, feat), F32)],
        compiler_params=params(),
        name="act_grad",
    )(gate_scale, up_scale, d_all, gate_q, up_q)

    act_part, d_w = lax.optimization_barrier((act_part, d_w))
    got_act = lax.all_to_all(act_part.reshape(n_col, tok // n_col, feat), "zl", 0, 0, tiled=True)
    gate_t, up_t, grad_act = pl.pallas_call(
        finish_kernel,
        grid=(n_x,),
        in_specs=[
            pl.BlockSpec((1, n_depth, rows, 2 * GROUP), lambda k: (k, 0, 0, 0)),
            pl.BlockSpec((n_depth, 1, rows, feat), lambda k: (0, k, 0, 0)),
            pl.BlockSpec((n_col, tok // n_col, feat), lambda k: (0, 0, 0)),
        ],
        out_specs=[
            pl.BlockSpec((slice_width, feat), lambda k: (0, 0)),
            pl.BlockSpec((slice_width, feat), lambda k: (0, 0)),
            pl.BlockSpec((tok // n_col, feat), lambda k: (0, 0)),
        ],
        out_shape=[
            jax.ShapeDtypeStruct((slice_width, feat), BF16),
            jax.ShapeDtypeStruct((slice_width, feat), BF16),
            jax.ShapeDtypeStruct((tok // n_col, feat), BF16),
        ],
        scratch_shapes=[pltpu.VMEM((2 * GROUP, feat), F32)],
        compiler_params=params(),
        name="finish",
    )(d_w, nat_all, got_act)
    return grad_act, gate_t.T, up_t.T


def solution(mesh):
    sizes = mesh.shape
    n_zh, n_core = 2, 2
    fine = Mesh(
        mesh.devices.reshape(
            sizes["depth"] // n_core, n_core, sizes["row"] // n_zh, n_zh, sizes["col"]
        ),
        ("y", "core", "x", "zh", "zl"),
    )
    depth, row, col = ("y", "core"), ("x", "zh"), "zl"
    return jax.shard_map(
        on_device,
        mesh=fine,
        in_specs=(
            P(depth, row),
            P(depth, row),
            P(depth, None),
            P(row, col),
            P(row, col),
            P(row, col),
            P(row, col),
            P(depth + row, col),
        ),
        out_specs=(
            P(depth + (col,), row),
            P(row, (col,) + depth),
            P(row, (col,) + depth),
        ),
        check_vma=False,
    )
```

```python
import jax
import jax.numpy as jnp
from jax import lax
from jax.experimental import pallas as pl
from jax.experimental.pallas import tpu as pltpu
from jax.sharding import Mesh
from jax.sharding import PartitionSpec as P

GROUP = 128
CHUNK = 256
F32 = jnp.float32
BF16 = jnp.bfloat16


def dequant(q_ref, s_ref, j):
    rows = []
    for r in range(q_ref.shape[0] // GROUP):
        tiles = []
        for g in range(j * CHUNK // GROUP, (j + 1) * CHUNK // GROUP):
            tile = q_ref[r * GROUP : (r + 1) * GROUP, g * GROUP : (g + 1) * GROUP].astype(F32)
            tiles.append((tile * s_ref[r, g]).astype(BF16))
        rows.append(jnp.concatenate(tiles, axis=1))
    return jnp.concatenate(rows, axis=0)


def chunk_copies(q_refs, w_ref, sems):
    return [
        [
            pltpu.make_async_copy(
                q.at[:, pl.ds(j * CHUNK, CHUNK)], w_ref.at[t, :, pl.ds(j * CHUNK, CHUNK)], sems.at[t, j]
            )
            for t, q in enumerate(q_refs)
        ]
        for j in range(w_ref.shape[2] // CHUNK)
    ]


def forward_kernel(
    gs_ref, us_ref, act_ref, ast_ref, order_ref, gq_ref, uq_ref, pre_ref, nat_ref, w_ref, sems
):
    copies = chunk_copies((gq_ref, uq_ref), w_ref, sems)
    for pair in copies:
        for copy in pair:
            copy.start()
    tok, feat = act_ref.shape
    one_hot = (
        lax.broadcasted_iota(jnp.int32, (tok, tok), 0)
        == jnp.broadcast_to(order_ref[...], (tok, tok))
    ).astype(F32).astype(BF16)
    parts = []
    for g in range(feat // GROUP):
        scale = jnp.broadcast_to(ast_ref[g : g + 1, :], (tok, tok)).T
        part = act_ref[:, g * GROUP : (g + 1) * GROUP].astype(F32) * scale
        parts.append(part.astype(BF16))
    scaled = jnp.concatenate(parts, axis=1)
    natural = jnp.dot(one_hot, scaled, preferred_element_type=F32).astype(BF16)
    nat_ref[...] = natural
    for j, pair in enumerate(copies):
        for t, s_ref in enumerate((gs_ref, us_ref)):
            pair[t].wait()
            w = dequant(w_ref.at[t], s_ref, j)
            out = jnp.dot(natural, w, preferred_element_type=F32).astype(BF16)
            pre_ref[:, j, t] = out.reshape(pre_ref.shape[0], pre_ref.shape[3], CHUNK)


def reduce_kernel(got_ref, out_ref):
    for j in range(out_ref.shape[0]):
        for t in range(2):
            total = got_ref[0, j, t].astype(F32)
            for i in range(1, got_ref.shape[0]):
                total += got_ref[i, j, t].astype(F32)
            out_ref[j, t] = total.astype(BF16)


def activation_kernel(zh_ref, pre_ref, own_ref, other_ref, d_ref, dp_ref, dg_ref, du_ref):
    first = zh_ref[0] == 0
    for j in range(pre_ref.shape[1]):
        cols = slice(j * CHUNK, (j + 1) * CHUNK)
        own, other = own_ref[:, cols].astype(F32), other_ref[:, cols].astype(F32)
        cot = jnp.concatenate(
            [jnp.where(first, own, other), jnp.where(first, other, own)], axis=0
        )
        gate = pre_ref[0, j, 0].astype(F32) + pre_ref[1, j, 0].astype(F32)
        up = pre_ref[0, j, 1].astype(F32) + pre_ref[1, j, 1].astype(F32)
        s = jax.nn.sigmoid(gate)
        d_gate = (cot * up * s * (1.0 + gate * (1.0 - s))).astype(BF16)
        d_up = (cot * gate * s).astype(BF16)
        d_ref[j, 0] = d_gate
        d_ref[j, 1] = d_up
        dg_ref[:, cols] = d_gate.astype(F32)
        du_ref[:, cols] = d_up.astype(F32)
    parts, width = dp_ref.shape[0], dg_ref.shape[1]
    step = width // parts
    for k in range(parts):
        base = (k * step) // GROUP * GROUP
        span = min(2 * GROUP, width - base)
        shift = k * step - base
        for t, src in enumerate((dg_ref, du_ref)):
            window = src[:, base : base + span]
            if shift:
                window = pltpu.roll(window, span - shift, 1)
            dp_ref[k, :, t * GROUP : (t + 1) * GROUP] = window[:, :GROUP].astype(BF16)


def act_grad_kernel(gs_ref, us_ref, d_ref, gq_ref, uq_ref, out_ref, w_ref, sems):
    copies = chunk_copies((gq_ref, uq_ref), w_ref, sems)
    for pair in copies:
        for copy in pair:
            copy.start()
    total = None
    for j, pair in enumerate(copies):
        for t, s_ref in enumerate((gs_ref, us_ref)):
            pair[t].wait()
            w = dequant(w_ref.at[t], s_ref, j)
            rows = d_ref[:, j, t].reshape(out_ref.shape[0], CHUNK)
            part = lax.dot_general(rows, w, (((1,), (1,)), ((), ())), preferred_element_type=F32)
            total = part if total is None else total + part
    out_ref[...] = total.astype(BF16)


def finish_kernel(dw_ref, nat_ref, got_ref, gate_ref, up_ref, act_ref):
    total = None
    for k in range(dw_ref.shape[0]):
        rows = dw_ref[k].reshape(dw_ref.shape[1] * dw_ref.shape[2], dw_ref.shape[3])
        nat = nat_ref[:, k].reshape(rows.shape[0], nat_ref.shape[3])
        part = lax.dot_general(rows, nat, (((0,), (0,)), ((), ())), preferred_element_type=F32)
        total = part if total is None else total + part
    width = gate_ref.shape[0]
    gate_ref[...] = total[:width].astype(BF16)
    up_ref[...] = total[GROUP : GROUP + width].astype(BF16)
    act_ref[...] = sum(got_ref[i].astype(F32) for i in range(got_ref.shape[0])).astype(BF16)


def params(mib):
    return pltpu.CompilerParams(vmem_limit_bytes=mib * 1024 * 1024)


def on_device(
    act_values, activation_scale, token_order, gate_q, gate_scale, up_q, up_scale, cotangent
):
    n_x, n_zh = lax.axis_size("x"), lax.axis_size("zh")
    n_depth = lax.axis_size("y") * lax.axis_size("core")
    n_col = lax.axis_size("zl")
    tok, feat = act_values.shape
    hidden = gate_q.shape[1]
    n_chunks = hidden // CHUNK
    rows = tok // n_x
    slice_width = hidden // n_depth
    smem = pl.BlockSpec(memory_space=pltpu.SMEM)
    vmem = pl.BlockSpec(memory_space=pltpu.VMEM)
    hbm = pl.BlockSpec(memory_space=pltpu.HBM)
    weights_scratch = [
        pltpu.VMEM((2, feat, hidden), BF16),
        pltpu.SemaphoreType.DMA((2, n_chunks)),
    ]

    cot_other = lax.ppermute(cotangent, "zh", [(i, (i + 1) % n_zh) for i in range(n_zh)])
    zh = lax.axis_index("zh").astype(jnp.int32)[None]

    pre, natural = pl.pallas_call(
        forward_kernel,
        in_specs=[smem, smem, vmem, vmem, vmem, hbm, hbm],
        out_specs=[vmem, vmem],
        out_shape=[
            jax.ShapeDtypeStruct((n_x, n_chunks, 2, rows, CHUNK), BF16),
            jax.ShapeDtypeStruct((tok, feat), BF16),
        ],
        scratch_shapes=weights_scratch,
        compiler_params=params(60),
        name="forward",
    )(gate_scale, up_scale, act_values, activation_scale.T, token_order, gate_q, up_q)

    nat_all = lax.all_gather(natural, ("y", "core"), axis=0, tiled=False)
    nat_all = nat_all.reshape(n_depth, n_x, rows, feat)

    got = lax.all_to_all(pre, "x", 0, 0, tiled=True)
    part = pl.pallas_call(
        reduce_kernel,
        in_specs=[vmem],
        out_specs=vmem,
        out_shape=jax.ShapeDtypeStruct((n_chunks, 2, rows, CHUNK), BF16),
        compiler_params=params(16),
        name="reduce",
    )(got)
    both = lax.all_gather(part, "zh", axis=0, tiled=False)

    d, d_split = pl.pallas_call(
        activation_kernel,
        in_specs=[smem, vmem, vmem, vmem],
        out_specs=[vmem, vmem],
        out_shape=[
            jax.ShapeDtypeStruct((n_chunks, 2, rows, CHUNK), BF16),
            jax.ShapeDtypeStruct((n_depth, rows, 2 * GROUP), BF16),
        ],
        scratch_shapes=[pltpu.VMEM((rows, hidden), F32), pltpu.VMEM((rows, hidden), F32)],
        compiler_params=params(16),
        name="activation",
    )(zh, both, cotangent, cot_other)

    d_all = lax.all_gather(d, "x", axis=0, tiled=False)
    d_depth = lax.all_to_all(d_split, ("y", "core"), 0, 0, tiled=True)
    d_all, nat_all, d_depth = lax.optimization_barrier((d_all, nat_all, d_depth))

    act_part = pl.pallas_call(
        act_grad_kernel,
        in_specs=[smem, smem, vmem, hbm, hbm],
        out_specs=vmem,
        out_shape=jax.ShapeDtypeStruct((tok, feat), BF16),
        scratch_shapes=weights_scratch,
        compiler_params=params(60),
        name="act_grad",
    )(gate_scale, up_scale, d_all, gate_q, up_q)

    d_copies = jnp.broadcast_to(d_depth[None], (n_x,) + d_depth.shape)
    d_w = lax.all_to_all(d_copies, "x", 0, 0, tiled=True)
    act_part, d_w = lax.optimization_barrier((act_part, d_w))
    got_act = lax.all_to_all(act_part.reshape(n_col, tok // n_col, feat), "zl", 0, 0, tiled=True)
    gate_t, up_t, grad_act = pl.pallas_call(
        finish_kernel,
        in_specs=[vmem] * 3,
        out_specs=[vmem] * 3,
        out_shape=[
            jax.ShapeDtypeStruct((slice_width, feat), BF16),
            jax.ShapeDtypeStruct((slice_width, feat), BF16),
            jax.ShapeDtypeStruct((tok // n_col, feat), BF16),
        ],
        compiler_params=params(16),
        name="finish",
    )(d_w, nat_all, got_act)
    return grad_act, gate_t.T, up_t.T


def solution(mesh):
    sizes = mesh.shape
    n_zh, n_core = 2, 2
    fine = Mesh(
        mesh.devices.reshape(
            sizes["depth"] // n_core, n_core, sizes["row"] // n_zh, n_zh, sizes["col"]
        ),
        ("y", "core", "x", "zh", "zl"),
    )
    depth, row, col = ("y", "core"), ("x", "zh"), "zl"
    return jax.shard_map(
        on_device,
        mesh=fine,
        in_specs=(
            P(depth, row),
            P(depth, row),
            P(depth, None),
            P(row, col),
            P(row, col),
            P(row, col),
            P(row, col),
            P(depth + row, col),
        ),
        out_specs=(
            P(depth + (col,), row),
            P(row, (col,) + depth),
            P(row, (col,) + depth),
        ),
        check_vma=False,
    )
```

```python
import jax
import jax.numpy as jnp
from jax import lax
from jax.experimental import pallas as pl
from jax.experimental.pallas import tpu as pltpu
from jax.sharding import Mesh
from jax.sharding import PartitionSpec as P

GROUP = 128
CHUNK = 256
AHEAD = 3
F32 = jnp.float32
BF16 = jnp.bfloat16


def dequant(q_ref, s_ref, j):
    rows = []
    for r in range(q_ref.shape[0] // GROUP):
        tiles = []
        for g in range(j * CHUNK // GROUP, (j + 1) * CHUNK // GROUP):
            tile = q_ref[r * GROUP : (r + 1) * GROUP, g * GROUP : (g + 1) * GROUP].astype(F32)
            tiles.append((tile * s_ref[r, g]).astype(BF16))
        rows.append(jnp.concatenate(tiles, axis=1))
    return jnp.concatenate(rows, axis=0)


def chunk_copies(q_refs, w_ref, sems):
    return [
        [
            pltpu.make_async_copy(
                q.at[:, pl.ds(j * CHUNK, CHUNK)], w_ref.at[t, :, pl.ds(j * CHUNK, CHUNK)], sems.at[t, j]
            )
            for t, q in enumerate(q_refs)
        ]
        for j in range(w_ref.shape[2] // CHUNK)
    ]


def all_copies(pairs, sems):
    copies = [pltpu.make_async_copy(src, dst, sems.at[i]) for i, (src, dst) in enumerate(pairs)]
    start(copies)
    return copies


def start(copies):
    for copy in copies:
        copy.start()


def wait(copies):
    for copy in copies:
        copy.wait()


def forward_kernel(
    gs_hbm, us_hbm, act_hbm, ast_hbm, order_hbm, gq_ref, uq_ref, pre_ref, nat_ref,
    gs_ref, us_ref, act_ref, ast_ref, order_ref, w_ref, sems, small_sems,
):
    small = all_copies(
        (
            (act_hbm, act_ref),
            (ast_hbm, ast_ref),
            (order_hbm, order_ref),
            (gs_hbm, gs_ref),
            (us_hbm, us_ref),
        ),
        small_sems,
    )
    copies = chunk_copies((gq_ref, uq_ref), w_ref, sems)
    for pair in copies[:AHEAD]:
        start(pair)
    wait(small)
    tok, feat = act_ref.shape
    one_hot = (
        lax.broadcasted_iota(jnp.int32, (tok, tok), 0)
        == jnp.broadcast_to(order_ref[...], (tok, tok))
    ).astype(F32).astype(BF16)
    parts = []
    for g in range(feat // GROUP):
        scale = jnp.broadcast_to(ast_ref[g : g + 1, :], (tok, tok)).T
        part = act_ref[:, g * GROUP : (g + 1) * GROUP].astype(F32) * scale
        parts.append(part.astype(BF16))
    scaled = jnp.concatenate(parts, axis=1)
    natural = jnp.dot(one_hot, scaled, preferred_element_type=F32).astype(BF16)
    nat_ref[...] = natural
    for j, pair in enumerate(copies):
        for t, s_ref in enumerate((gs_ref, us_ref)):
            pair[t].wait()
            w = dequant(w_ref.at[t], s_ref, j)
            out = jnp.dot(natural, w, preferred_element_type=F32).astype(BF16)
            pre_ref[:, j, t] = out.reshape(pre_ref.shape[0], pre_ref.shape[3], CHUNK)
        if j + AHEAD < len(copies):
            start(copies[j + AHEAD])


def reduce_kernel(got_ref, out_ref):
    for j in range(out_ref.shape[0]):
        for t in range(2):
            total = got_ref[0, j, t].astype(F32)
            for i in range(1, got_ref.shape[0]):
                total += got_ref[i, j, t].astype(F32)
            out_ref[j, t] = total.astype(BF16)


def activation_kernel(zh_ref, pre_ref, own_ref, other_ref, d_ref, dp_ref, dg_ref, du_ref):
    first = zh_ref[0] == 0
    for j in range(pre_ref.shape[1]):
        cols = slice(j * CHUNK, (j + 1) * CHUNK)
        own, other = own_ref[:, cols].astype(F32), other_ref[:, cols].astype(F32)
        cot = jnp.concatenate(
            [jnp.where(first, own, other), jnp.where(first, other, own)], axis=0
        )
        gate = pre_ref[0, j, 0].astype(F32) + pre_ref[1, j, 0].astype(F32)
        up = pre_ref[0, j, 1].astype(F32) + pre_ref[1, j, 1].astype(F32)
        s = jax.nn.sigmoid(gate)
        d_gate = (cot * up * s * (1.0 + gate * (1.0 - s))).astype(BF16)
        d_up = (cot * gate * s).astype(BF16)
        d_ref[j, 0] = d_gate
        d_ref[j, 1] = d_up
        dg_ref[:, cols] = d_gate.astype(F32)
        du_ref[:, cols] = d_up.astype(F32)
    parts, width = dp_ref.shape[0], dg_ref.shape[1]
    step = width // parts
    for k in range(parts):
        base = (k * step) // GROUP * GROUP
        span = min(2 * GROUP, width - base)
        shift = k * step - base
        for t, src in enumerate((dg_ref, du_ref)):
            window = src[:, base : base + span]
            if shift:
                window = pltpu.roll(window, span - shift, 1)
            dp_ref[k, :, t * GROUP : (t + 1) * GROUP] = window[:, :GROUP].astype(BF16)


def act_grad_kernel(
    gs_hbm, us_hbm, d_hbm, gq_ref, uq_ref, out_ref, gs_ref, us_ref, d_ref, w_ref, sems, small_sems
):
    small = all_copies(((gs_hbm, gs_ref), (us_hbm, us_ref)), small_sems)
    copies = chunk_copies((gq_ref, uq_ref), w_ref, sems)
    for j, pair in enumerate(copies):
        pair.append(pltpu.make_async_copy(d_hbm.at[:, j], d_ref.at[:, j], sems.at[2, j]))
        start(pair)
    wait(small)
    total = None
    for j, (*pair, d_copy) in enumerate(copies):
        d_copy.wait()
        for t, s_ref in enumerate((gs_ref, us_ref)):
            pair[t].wait()
            w = dequant(w_ref.at[t], s_ref, j)
            rows = d_ref[:, j, t].reshape(out_ref.shape[0], CHUNK)
            part = lax.dot_general(rows, w, (((1,), (1,)), ((), ())), preferred_element_type=F32)
            total = part if total is None else total + part
    out_ref[...] = total.astype(BF16)


def finish_kernel(dw_ref, nat_ref, got_ref, gate_ref, up_ref, act_ref):
    total = None
    for k in range(dw_ref.shape[0]):
        rows = dw_ref[k].reshape(dw_ref.shape[1] * dw_ref.shape[2], dw_ref.shape[3])
        nat = nat_ref[:, k].reshape(rows.shape[0], nat_ref.shape[3])
        part = lax.dot_general(rows, nat, (((0,), (0,)), ((), ())), preferred_element_type=F32)
        total = part if total is None else total + part
    width = gate_ref.shape[0]
    gate_ref[...] = total[:width].astype(BF16)
    up_ref[...] = total[GROUP : GROUP + width].astype(BF16)
    act_ref[...] = sum(got_ref[i].astype(F32) for i in range(got_ref.shape[0])).astype(BF16)


def params(mib):
    return pltpu.CompilerParams(vmem_limit_bytes=mib * 1024 * 1024)


def on_device(
    act_values, activation_scale, token_order, gate_q, gate_scale, up_q, up_scale, cotangent
):
    n_x, n_zh = lax.axis_size("x"), lax.axis_size("zh")
    n_depth = lax.axis_size("y") * lax.axis_size("core")
    n_col = lax.axis_size("zl")
    tok, feat = act_values.shape
    hidden = gate_q.shape[1]
    n_chunks = hidden // CHUNK
    rows = tok // n_x
    slice_width = hidden // n_depth
    smem = pl.BlockSpec(memory_space=pltpu.SMEM)
    vmem = pl.BlockSpec(memory_space=pltpu.VMEM)
    hbm = pl.BlockSpec(memory_space=pltpu.HBM)
    scale_scratch = [pltpu.SMEM(gate_scale.shape, F32), pltpu.SMEM(up_scale.shape, F32)]
    weights_scratch = pltpu.VMEM((2, feat, hidden), BF16)

    cot_other = lax.ppermute(cotangent, "zh", [(i, (i + 1) % n_zh) for i in range(n_zh)])
    zh = lax.axis_index("zh").astype(jnp.int32)[None]

    pre, natural = pl.pallas_call(
        forward_kernel,
        in_specs=[hbm] * 7,
        out_specs=[vmem, vmem],
        out_shape=[
            jax.ShapeDtypeStruct((n_x, n_chunks, 2, rows, CHUNK), BF16),
            jax.ShapeDtypeStruct((tok, feat), BF16),
        ],
        scratch_shapes=[
            *scale_scratch,
            pltpu.VMEM((tok, feat), BF16),
            pltpu.VMEM((feat // GROUP, tok), F32),
            pltpu.VMEM((1, tok), jnp.int32),
            weights_scratch,
            pltpu.SemaphoreType.DMA((2, n_chunks)),
            pltpu.SemaphoreType.DMA((5,)),
        ],
        compiler_params=params(60),
        name="forward",
    )(gate_scale, up_scale, act_values, activation_scale.T, token_order, gate_q, up_q)

    nat_all = lax.all_gather(natural, ("y", "core"), axis=0, tiled=False)
    nat_all = nat_all.reshape(n_depth, n_x, rows, feat)

    got = lax.all_to_all(pre, "x", 0, 0, tiled=True)
    part = pl.pallas_call(
        reduce_kernel,
        in_specs=[vmem],
        out_specs=vmem,
        out_shape=jax.ShapeDtypeStruct((n_chunks, 2, rows, CHUNK), BF16),
        compiler_params=params(16),
        name="reduce",
    )(got)
    both = lax.all_gather(part, "zh", axis=0, tiled=False)

    d, d_split = pl.pallas_call(
        activation_kernel,
        in_specs=[smem, vmem, vmem, vmem],
        out_specs=[vmem, vmem],
        out_shape=[
            jax.ShapeDtypeStruct((n_chunks, 2, rows, CHUNK), BF16),
            jax.ShapeDtypeStruct((n_depth, rows, 2 * GROUP), BF16),
        ],
        scratch_shapes=[pltpu.VMEM((rows, hidden), F32), pltpu.VMEM((rows, hidden), F32)],
        compiler_params=params(16),
        name="activation",
    )(zh, both, cotangent, cot_other)

    d_all = lax.all_gather(d, "x", axis=0, tiled=False)
    d_depth = lax.all_to_all(d_split, ("y", "core"), 0, 0, tiled=True)
    d_all, nat_all, d_depth = lax.optimization_barrier((d_all, nat_all, d_depth))

    act_part = pl.pallas_call(
        act_grad_kernel,
        in_specs=[hbm] * 5,
        out_specs=vmem,
        out_shape=jax.ShapeDtypeStruct((tok, feat), BF16),
        scratch_shapes=[
            *scale_scratch,
            pltpu.VMEM((n_x, n_chunks, 2, rows, CHUNK), BF16),
            weights_scratch,
            pltpu.SemaphoreType.DMA((3, n_chunks)),
            pltpu.SemaphoreType.DMA((2,)),
        ],
        compiler_params=params(60),
        name="act_grad",
    )(gate_scale, up_scale, d_all, gate_q, up_q)

    d_copies = jnp.broadcast_to(d_depth[None], (n_x,) + d_depth.shape)
    d_w = lax.all_to_all(d_copies, "x", 0, 0, tiled=True)
    act_part, d_w = lax.optimization_barrier((act_part, d_w))
    got_act = lax.all_to_all(act_part.reshape(n_col, tok // n_col, feat), "zl", 0, 0, tiled=True)
    gate_t, up_t, grad_act = pl.pallas_call(
        finish_kernel,
        in_specs=[vmem] * 3,
        out_specs=[vmem] * 3,
        out_shape=[
            jax.ShapeDtypeStruct((slice_width, feat), BF16),
            jax.ShapeDtypeStruct((slice_width, feat), BF16),
            jax.ShapeDtypeStruct((tok // n_col, feat), BF16),
        ],
        compiler_params=params(16),
        name="finish",
    )(d_w, nat_all, got_act)
    return grad_act, gate_t.T, up_t.T


def solution(mesh):
    sizes = mesh.shape
    n_zh, n_core = 2, 2
    fine = Mesh(
        mesh.devices.reshape(
            sizes["depth"] // n_core, n_core, sizes["row"] // n_zh, n_zh, sizes["col"]
        ),
        ("y", "core", "x", "zh", "zl"),
    )
    depth, row, col = ("y", "core"), ("x", "zh"), "zl"
    return jax.shard_map(
        on_device,
        mesh=fine,
        in_specs=(
            P(depth, row),
            P(depth, row),
            P(depth, None),
            P(row, col),
            P(row, col),
            P(row, col),
            P(row, col),
            P(depth + row, col),
        ),
        out_specs=(
            P(depth + (col,), row),
            P(row, (col,) + depth),
            P(row, (col,) + depth),
        ),
        check_vma=False,
    )
```

```python
import jax
import jax.numpy as jnp
from jax import lax
from jax.experimental import pallas as pl
from jax.experimental.pallas import tpu as pltpu
from jax.sharding import Mesh
from jax.sharding import PartitionSpec as P

GROUP = 128
CHUNK = 256
AHEAD = 3
F32 = jnp.float32
BF16 = jnp.bfloat16


def dequant(q_ref, s_ref, j):
    rows = []
    for r in range(q_ref.shape[0] // GROUP):
        tiles = []
        for g in range(j * CHUNK // GROUP, (j + 1) * CHUNK // GROUP):
            tile = q_ref[r * GROUP : (r + 1) * GROUP, g * GROUP : (g + 1) * GROUP].astype(F32)
            tiles.append((tile * s_ref[r, g]).astype(BF16))
        rows.append(jnp.concatenate(tiles, axis=1))
    return jnp.concatenate(rows, axis=0)


def chunk_copies(q_refs, w_ref, sems):
    return [
        [
            pltpu.make_async_copy(
                q.at[:, pl.ds(j * CHUNK, CHUNK)], w_ref.at[t, :, pl.ds(j * CHUNK, CHUNK)], sems.at[t, j]
            )
            for t, q in enumerate(q_refs)
        ]
        for j in range(w_ref.shape[2] // CHUNK)
    ]


def all_copies(pairs, sems):
    copies = [pltpu.make_async_copy(src, dst, sems.at[i]) for i, (src, dst) in enumerate(pairs)]
    start(copies)
    return copies


def start(copies):
    for copy in copies:
        copy.start()


def wait(copies):
    for copy in copies:
        copy.wait()


def forward_kernel(
    gs_hbm, us_hbm, act_hbm, ast_hbm, order_hbm, gq_ref, uq_ref, pre_ref, nat_ref,
    gs_ref, us_ref, act_ref, ast_ref, order_ref, w_ref, sems, small_sems,
):
    small = all_copies(
        (
            (act_hbm, act_ref),
            (ast_hbm, ast_ref),
            (order_hbm, order_ref),
            (gs_hbm, gs_ref),
            (us_hbm, us_ref),
        ),
        small_sems,
    )
    copies = chunk_copies((gq_ref, uq_ref), w_ref, sems)
    for pair in copies[:AHEAD]:
        start(pair)
    wait(small)
    tok, feat = act_ref.shape
    one_hot = (
        lax.broadcasted_iota(jnp.int32, (tok, tok), 0)
        == jnp.broadcast_to(order_ref[...], (tok, tok))
    ).astype(F32).astype(BF16)
    parts = []
    for g in range(feat // GROUP):
        scale = jnp.broadcast_to(ast_ref[g : g + 1, :], (tok, tok)).T
        part = act_ref[:, g * GROUP : (g + 1) * GROUP].astype(F32) * scale
        parts.append(part.astype(BF16))
    scaled = jnp.concatenate(parts, axis=1)
    natural = jnp.dot(one_hot, scaled, preferred_element_type=F32).astype(BF16)
    nat_ref[...] = natural
    for j, pair in enumerate(copies):
        for t, s_ref in enumerate((gs_ref, us_ref)):
            pair[t].wait()
            w = dequant(w_ref.at[t], s_ref, j)
            out = jnp.dot(natural, w, preferred_element_type=F32).astype(BF16)
            pre_ref[:, j, t] = out.reshape(pre_ref.shape[0], pre_ref.shape[3], CHUNK)
        if j + AHEAD < len(copies):
            start(copies[j + AHEAD])


def reduce_kernel(got_ref, out_ref):
    for j in range(out_ref.shape[0]):
        for t in range(2):
            total = got_ref[0, j, t].astype(F32)
            for i in range(1, got_ref.shape[0]):
                total += got_ref[i, j, t].astype(F32)
            out_ref[j, t] = total.astype(BF16)


def activation_kernel(zh_ref, pre_ref, own_ref, other_ref, d_ref, dp_ref, dg_ref, du_ref):
    first = zh_ref[0] == 0
    for j in range(pre_ref.shape[1]):
        cols = slice(j * CHUNK, (j + 1) * CHUNK)
        own, other = own_ref[:, cols].astype(F32), other_ref[:, cols].astype(F32)
        cot = jnp.concatenate(
            [jnp.where(first, own, other), jnp.where(first, other, own)], axis=0
        )
        gate = pre_ref[0, j, 0].astype(F32) + pre_ref[1, j, 0].astype(F32)
        up = pre_ref[0, j, 1].astype(F32) + pre_ref[1, j, 1].astype(F32)
        s = jax.nn.sigmoid(gate)
        d_gate = (cot * up * s * (1.0 + gate * (1.0 - s))).astype(BF16)
        d_up = (cot * gate * s).astype(BF16)
        d_ref[j, 0] = d_gate
        d_ref[j, 1] = d_up
        dg_ref[:, cols] = d_gate.astype(F32)
        du_ref[:, cols] = d_up.astype(F32)
    parts, width = dp_ref.shape[0], dg_ref.shape[1]
    step = width // parts
    for k in range(parts):
        base = (k * step) // GROUP * GROUP
        span = min(2 * GROUP, width - base)
        shift = k * step - base
        for t, src in enumerate((dg_ref, du_ref)):
            window = src[:, base : base + span]
            if shift:
                window = pltpu.roll(window, span - shift, 1)
            dp_ref[k, :, t * GROUP : (t + 1) * GROUP] = window[:, :GROUP].astype(BF16)


def act_grad_kernel(
    gs_hbm, us_hbm, d_hbm, gq_ref, uq_ref, out_ref, gs_ref, us_ref, d_ref, w_ref, sems, small_sems
):
    small = all_copies(((gs_hbm, gs_ref), (us_hbm, us_ref)), small_sems)
    copies = chunk_copies((gq_ref, uq_ref), w_ref, sems)
    for j, pair in enumerate(copies):
        pair.append(pltpu.make_async_copy(d_hbm.at[:, j], d_ref.at[:, j], sems.at[2, j]))
        start(pair)
    wait(small)
    total = None
    for j, (*pair, d_copy) in enumerate(copies):
        d_copy.wait()
        for t, s_ref in enumerate((gs_ref, us_ref)):
            pair[t].wait()
            w = dequant(w_ref.at[t], s_ref, j)
            rows = d_ref[:, j, t].reshape(out_ref.shape[0], CHUNK)
            part = lax.dot_general(rows, w, (((1,), (1,)), ((), ())), preferred_element_type=F32)
            total = part if total is None else total + part
    out_ref[...] = total.astype(BF16)


def finish_kernel(dw_ref, nat_ref, got_ref, gate_ref, up_ref, act_ref):
    total = None
    for k in range(dw_ref.shape[0]):
        rows = dw_ref[k].reshape(dw_ref.shape[1] * dw_ref.shape[2], dw_ref.shape[3])
        nat = nat_ref[:, k].reshape(rows.shape[0], nat_ref.shape[3])
        part = lax.dot_general(rows, nat, (((0,), (0,)), ((), ())), preferred_element_type=F32)
        total = part if total is None else total + part
    width = gate_ref.shape[0]
    gate_ref[...] = total[:width].astype(BF16)
    up_ref[...] = total[GROUP : GROUP + width].astype(BF16)
    act_ref[...] = sum(got_ref[i].astype(F32) for i in range(got_ref.shape[0])).astype(BF16)


def params(mib):
    return pltpu.CompilerParams(vmem_limit_bytes=mib * 1024 * 1024)


def on_device(
    act_values, activation_scale, token_order, gate_q, gate_scale, up_q, up_scale, cotangent
):
    n_x, n_zh = lax.axis_size("x"), lax.axis_size("zh")
    n_depth = lax.axis_size("y") * lax.axis_size("core")
    n_col = lax.axis_size("zl")
    tok, feat = act_values.shape
    hidden = gate_q.shape[1]
    n_chunks = hidden // CHUNK
    rows = tok // n_x
    slice_width = hidden // n_depth
    smem = pl.BlockSpec(memory_space=pltpu.SMEM)
    vmem = pl.BlockSpec(memory_space=pltpu.VMEM)
    hbm = pl.BlockSpec(memory_space=pltpu.HBM)
    scale_scratch = [pltpu.SMEM(gate_scale.shape, F32), pltpu.SMEM(up_scale.shape, F32)]
    weights_scratch = pltpu.VMEM((2, feat, hidden), BF16)

    cot_other = lax.ppermute(cotangent, "zh", [(i, (i + 1) % n_zh) for i in range(n_zh)])
    zh = lax.axis_index("zh").astype(jnp.int32)[None]

    pre, natural = pl.pallas_call(
        forward_kernel,
        in_specs=[hbm] * 7,
        out_specs=[vmem, vmem],
        out_shape=[
            jax.ShapeDtypeStruct((n_x, n_chunks, 2, rows, CHUNK), BF16),
            jax.ShapeDtypeStruct((tok, feat), BF16),
        ],
        scratch_shapes=[
            *scale_scratch,
            pltpu.VMEM((tok, feat), BF16),
            pltpu.VMEM((feat // GROUP, tok), F32),
            pltpu.VMEM((1, tok), jnp.int32),
            weights_scratch,
            pltpu.SemaphoreType.DMA((2, n_chunks)),
            pltpu.SemaphoreType.DMA((5,)),
        ],
        compiler_params=params(60),
        name="forward",
    )(gate_scale, up_scale, act_values, activation_scale.T, token_order, gate_q, up_q)

    nat_all = lax.all_gather(natural, ("y", "core"), axis=0, tiled=False)
    nat_all = nat_all.reshape(n_depth, n_x, rows, feat)

    got = lax.all_to_all(pre, "x", 0, 0, tiled=True)
    part = pl.pallas_call(
        reduce_kernel,
        in_specs=[vmem],
        out_specs=vmem,
        out_shape=jax.ShapeDtypeStruct((n_chunks, 2, rows, CHUNK), BF16),
        compiler_params=params(16),
        name="reduce",
    )(got)
    both = lax.all_gather(part, "zh", axis=0, tiled=False)

    d, d_split = pl.pallas_call(
        activation_kernel,
        in_specs=[smem, vmem, vmem, vmem],
        out_specs=[vmem, vmem],
        out_shape=[
            jax.ShapeDtypeStruct((n_chunks, 2, rows, CHUNK), BF16),
            jax.ShapeDtypeStruct((n_depth, rows, 2 * GROUP), BF16),
        ],
        scratch_shapes=[pltpu.VMEM((rows, hidden), F32), pltpu.VMEM((rows, hidden), F32)],
        compiler_params=params(16),
        name="activation",
    )(zh, both, cotangent, cot_other)

    d_all = lax.all_gather(d, "x", axis=0, tiled=False)
    d_depth = lax.all_to_all(d_split, ("y", "core"), 0, 0, tiled=True)
    d_all, nat_all, d_depth = lax.optimization_barrier((d_all, nat_all, d_depth))
    d_w = lax.all_gather(d_depth, "x", axis=0, tiled=False)

    act_part = pl.pallas_call(
        act_grad_kernel,
        in_specs=[hbm] * 5,
        out_specs=vmem,
        out_shape=jax.ShapeDtypeStruct((tok, feat), BF16),
        scratch_shapes=[
            *scale_scratch,
            pltpu.VMEM((n_x, n_chunks, 2, rows, CHUNK), BF16),
            weights_scratch,
            pltpu.SemaphoreType.DMA((3, n_chunks)),
            pltpu.SemaphoreType.DMA((2,)),
        ],
        compiler_params=params(60),
        name="act_grad",
    )(gate_scale, up_scale, d_all, gate_q, up_q)

    got_act = lax.all_to_all(act_part.reshape(n_col, tok // n_col, feat), "zl", 0, 0, tiled=True)
    gate_t, up_t, grad_act = pl.pallas_call(
        finish_kernel,
        in_specs=[vmem] * 3,
        out_specs=[vmem] * 3,
        out_shape=[
            jax.ShapeDtypeStruct((slice_width, feat), BF16),
            jax.ShapeDtypeStruct((slice_width, feat), BF16),
            jax.ShapeDtypeStruct((tok // n_col, feat), BF16),
        ],
        compiler_params=params(16),
        name="finish",
    )(d_w, nat_all, got_act)
    return grad_act, gate_t.T, up_t.T


def solution(mesh):
    sizes = mesh.shape
    n_zh, n_core = 2, 2
    fine = Mesh(
        mesh.devices.reshape(
            sizes["depth"] // n_core, n_core, sizes["row"] // n_zh, n_zh, sizes["col"]
        ),
        ("y", "core", "x", "zh", "zl"),
    )
    depth, row, col = ("y", "core"), ("x", "zh"), "zl"
    return jax.shard_map(
        on_device,
        mesh=fine,
        in_specs=(
            P(depth, row),
            P(depth, row),
            P(depth, None),
            P(row, col),
            P(row, col),
            P(row, col),
            P(row, col),
            P(depth + row, col),
        ),
        out_specs=(
            P(depth + (col,), row),
            P(row, (col,) + depth),
            P(row, (col,) + depth),
        ),
        check_vma=False,
    )
```

```python
import jax
import jax.numpy as jnp
from jax import lax
from jax.experimental import pallas as pl
from jax.experimental.pallas import tpu as pltpu
from jax.sharding import Mesh
from jax.sharding import PartitionSpec as P

GROUP = 128
CHUNK = 256
AHEAD = 3
F32 = jnp.float32
BF16 = jnp.bfloat16


def dequant(q_ref, s_ref, j):
    rows = []
    for r in range(q_ref.shape[0] // GROUP):
        tiles = []
        for g in range(j * CHUNK // GROUP, (j + 1) * CHUNK // GROUP):
            tile = q_ref[r * GROUP : (r + 1) * GROUP, g * GROUP : (g + 1) * GROUP].astype(F32)
            tiles.append((tile * s_ref[r, g]).astype(BF16))
        rows.append(jnp.concatenate(tiles, axis=1))
    return jnp.concatenate(rows, axis=0)


def chunk_copies(q_refs, w_ref, sems):
    return [
        [
            pltpu.make_async_copy(
                q.at[:, pl.ds(j * CHUNK, CHUNK)], w_ref.at[t, :, pl.ds(j * CHUNK, CHUNK)], sems.at[t, j]
            )
            for t, q in enumerate(q_refs)
        ]
        for j in range(w_ref.shape[2] // CHUNK)
    ]


def all_copies(pairs, sems):
    copies = [pltpu.make_async_copy(src, dst, sems.at[i]) for i, (src, dst) in enumerate(pairs)]
    start(copies)
    return copies


def start(copies):
    for copy in copies:
        copy.start()


def wait(copies):
    for copy in copies:
        copy.wait()


def forward_kernel(
    gs_hbm, us_hbm, act_hbm, ast_hbm, order_hbm, gq_ref, uq_ref, pre_ref, nat_ref,
    gs_ref, us_ref, act_ref, ast_ref, order_ref, w_ref, sems, small_sems,
):
    small = all_copies(
        (
            (act_hbm, act_ref),
            (ast_hbm, ast_ref),
            (order_hbm, order_ref),
            (gs_hbm, gs_ref),
            (us_hbm, us_ref),
        ),
        small_sems,
    )
    copies = chunk_copies((gq_ref, uq_ref), w_ref, sems)
    for pair in copies[:AHEAD]:
        start(pair)
    wait(small)
    tok, feat = act_ref.shape
    one_hot = (
        lax.broadcasted_iota(jnp.int32, (tok, tok), 0)
        == jnp.broadcast_to(order_ref[...], (tok, tok))
    ).astype(F32).astype(BF16)
    parts = []
    for g in range(feat // GROUP):
        scale = jnp.broadcast_to(ast_ref[g : g + 1, :], (tok, tok)).T
        part = act_ref[:, g * GROUP : (g + 1) * GROUP].astype(F32) * scale
        parts.append(part.astype(BF16))
    scaled = jnp.concatenate(parts, axis=1)
    natural = jnp.dot(one_hot, scaled, preferred_element_type=F32).astype(BF16)
    nat_ref[...] = natural
    for j, pair in enumerate(copies):
        for t, s_ref in enumerate((gs_ref, us_ref)):
            pair[t].wait()
            w = dequant(w_ref.at[t], s_ref, j)
            out = jnp.dot(natural, w, preferred_element_type=F32).astype(BF16)
            pre_ref[:, j, t] = out.reshape(pre_ref.shape[0], pre_ref.shape[3], CHUNK)
        if j + AHEAD < len(copies):
            start(copies[j + AHEAD])


def reduce_kernel(got_ref, out_ref):
    for j in range(out_ref.shape[0]):
        for t in range(2):
            total = got_ref[0, j, t].astype(F32)
            for i in range(1, got_ref.shape[0]):
                total += got_ref[i, j, t].astype(F32)
            out_ref[j, t] = total.astype(BF16)


def activation_kernel(zh_ref, pre_ref, own_ref, other_ref, d_ref, dp_ref, dg_ref, du_ref):
    first = zh_ref[0] == 0
    for j in range(pre_ref.shape[1]):
        cols = slice(j * CHUNK, (j + 1) * CHUNK)
        own, other = own_ref[:, cols].astype(F32), other_ref[:, cols].astype(F32)
        cot = jnp.concatenate(
            [jnp.where(first, own, other), jnp.where(first, other, own)], axis=0
        )
        gate = pre_ref[0, j, 0].astype(F32) + pre_ref[1, j, 0].astype(F32)
        up = pre_ref[0, j, 1].astype(F32) + pre_ref[1, j, 1].astype(F32)
        s = jax.nn.sigmoid(gate)
        d_gate = (cot * up * s * (1.0 + gate * (1.0 - s))).astype(BF16)
        d_up = (cot * gate * s).astype(BF16)
        d_ref[j, 0] = d_gate
        d_ref[j, 1] = d_up
        dg_ref[:, cols] = d_gate.astype(F32)
        du_ref[:, cols] = d_up.astype(F32)
    parts, width = dp_ref.shape[0], dg_ref.shape[1]
    step = width // parts
    for k in range(parts):
        base = (k * step) // GROUP * GROUP
        span = min(2 * GROUP, width - base)
        shift = k * step - base
        for t, src in enumerate((dg_ref, du_ref)):
            window = src[:, base : base + span]
            if shift:
                window = pltpu.roll(window, span - shift, 1)
            dp_ref[k, :, t * GROUP : (t + 1) * GROUP] = window[:, :GROUP].astype(BF16)


def act_grad_kernel(
    gs_hbm, us_hbm, d_hbm, gq_ref, uq_ref, out_ref, gs_ref, us_ref, d_ref, w_ref, sems, small_sems
):
    small = all_copies(((gs_hbm, gs_ref), (us_hbm, us_ref)), small_sems)
    copies = chunk_copies((gq_ref, uq_ref), w_ref, sems)
    for j, pair in enumerate(copies):
        pair.append(pltpu.make_async_copy(d_hbm.at[:, j], d_ref.at[:, j], sems.at[2, j]))
        start(pair)
    wait(small)
    total = None
    for j, (*pair, d_copy) in enumerate(copies):
        d_copy.wait()
        for t, s_ref in enumerate((gs_ref, us_ref)):
            pair[t].wait()
            w = dequant(w_ref.at[t], s_ref, j)
            rows = d_ref[:, j, t].reshape(out_ref.shape[0], CHUNK)
            part = lax.dot_general(rows, w, (((1,), (1,)), ((), ())), preferred_element_type=F32)
            total = part if total is None else total + part
    out_ref[...] = total.astype(BF16)


def finish_kernel(dw_ref, nat_ref, got_ref, gate_ref, up_ref, act_ref):
    total = None
    for k in range(dw_ref.shape[0]):
        rows = dw_ref[k].reshape(dw_ref.shape[1] * dw_ref.shape[2], dw_ref.shape[3])
        nat = nat_ref[:, k].reshape(rows.shape[0], nat_ref.shape[3])
        part = lax.dot_general(rows, nat, (((0,), (0,)), ((), ())), preferred_element_type=F32)
        total = part if total is None else total + part
    width = gate_ref.shape[0]
    gate_ref[...] = total[:width].astype(BF16)
    up_ref[...] = total[GROUP : GROUP + width].astype(BF16)
    act_ref[...] = sum(got_ref[i].astype(F32) for i in range(got_ref.shape[0])).astype(BF16)


def params(mib):
    return pltpu.CompilerParams(vmem_limit_bytes=mib * 1024 * 1024)


def on_device(
    act_values, activation_scale, token_order, gate_q, gate_scale, up_q, up_scale, cotangent
):
    n_x, n_zh = lax.axis_size("x"), lax.axis_size("zh")
    n_depth = lax.axis_size("y") * lax.axis_size("core")
    n_col = lax.axis_size("zl")
    tok, feat = act_values.shape
    hidden = gate_q.shape[1]
    n_chunks = hidden // CHUNK
    rows = tok // n_x
    slice_width = hidden // n_depth
    smem = pl.BlockSpec(memory_space=pltpu.SMEM)
    vmem = pl.BlockSpec(memory_space=pltpu.VMEM)
    hbm = pl.BlockSpec(memory_space=pltpu.HBM)
    scale_scratch = [pltpu.SMEM(gate_scale.shape, F32), pltpu.SMEM(up_scale.shape, F32)]
    weights_scratch = pltpu.VMEM((2, feat, hidden), BF16)

    cot_other = lax.ppermute(cotangent, "zh", [(i, (i + 1) % n_zh) for i in range(n_zh)])
    zh = lax.axis_index("zh").astype(jnp.int32)[None]

    pre, natural = pl.pallas_call(
        forward_kernel,
        in_specs=[hbm] * 7,
        out_specs=[vmem, vmem],
        out_shape=[
            jax.ShapeDtypeStruct((n_x, n_chunks, 2, rows, CHUNK), BF16),
            jax.ShapeDtypeStruct((tok, feat), BF16),
        ],
        scratch_shapes=[
            *scale_scratch,
            pltpu.VMEM((tok, feat), BF16),
            pltpu.VMEM((feat // GROUP, tok), F32),
            pltpu.VMEM((1, tok), jnp.int32),
            weights_scratch,
            pltpu.SemaphoreType.DMA((2, n_chunks)),
            pltpu.SemaphoreType.DMA((5,)),
        ],
        compiler_params=params(60),
        name="forward",
    )(gate_scale, up_scale, act_values, activation_scale.T, token_order, gate_q, up_q)

    nat_all = lax.all_gather(natural, ("y", "core"), axis=0, tiled=False)
    nat_all = nat_all.reshape(n_depth, n_x, rows, feat)

    got = lax.all_to_all(pre, "x", 0, 0, tiled=True)
    part = pl.pallas_call(
        reduce_kernel,
        in_specs=[vmem],
        out_specs=vmem,
        out_shape=jax.ShapeDtypeStruct((n_chunks, 2, rows, CHUNK), BF16),
        compiler_params=params(16),
        name="reduce",
    )(got)
    both = lax.all_gather(part, "zh", axis=0, tiled=False)

    d, d_split = pl.pallas_call(
        activation_kernel,
        in_specs=[smem, vmem, vmem, vmem],
        out_specs=[vmem, vmem],
        out_shape=[
            jax.ShapeDtypeStruct((n_chunks, 2, rows, CHUNK), BF16),
            jax.ShapeDtypeStruct((n_depth, rows, 2 * GROUP), BF16),
        ],
        scratch_shapes=[pltpu.VMEM((rows, hidden), F32), pltpu.VMEM((rows, hidden), F32)],
        compiler_params=params(16),
        name="activation",
    )(zh, both, cotangent, cot_other)

    d_all = lax.all_gather(d, "x", axis=0, tiled=False)
    d_depth = lax.all_to_all(d_split, ("y", "core"), 0, 0, tiled=True)
    d_all, nat_all = lax.optimization_barrier((d_all, nat_all))

    act_part = pl.pallas_call(
        act_grad_kernel,
        in_specs=[hbm] * 5,
        out_specs=vmem,
        out_shape=jax.ShapeDtypeStruct((tok, feat), BF16),
        scratch_shapes=[
            *scale_scratch,
            pltpu.VMEM((n_x, n_chunks, 2, rows, CHUNK), BF16),
            weights_scratch,
            pltpu.SemaphoreType.DMA((3, n_chunks)),
            pltpu.SemaphoreType.DMA((2,)),
        ],
        compiler_params=params(60),
        name="act_grad",
    )(gate_scale, up_scale, d_all, gate_q, up_q)

    d_copies = jnp.broadcast_to(d_depth[None], (n_x,) + d_depth.shape)
    d_w = lax.all_to_all(d_copies, "x", 0, 0, tiled=True)
    got_act = lax.all_to_all(act_part.reshape(n_col, tok // n_col, feat), "zl", 0, 0, tiled=True)
    gate_t, up_t, grad_act = pl.pallas_call(
        finish_kernel,
        in_specs=[vmem] * 3,
        out_specs=[vmem] * 3,
        out_shape=[
            jax.ShapeDtypeStruct((slice_width, feat), BF16),
            jax.ShapeDtypeStruct((slice_width, feat), BF16),
            jax.ShapeDtypeStruct((tok // n_col, feat), BF16),
        ],
        compiler_params=params(16),
        name="finish",
    )(d_w, nat_all, got_act)
    return grad_act, gate_t.T, up_t.T


def solution(mesh):
    sizes = mesh.shape
    n_zh, n_core = 2, 2
    fine = Mesh(
        mesh.devices.reshape(
            sizes["depth"] // n_core, n_core, sizes["row"] // n_zh, n_zh, sizes["col"]
        ),
        ("y", "core", "x", "zh", "zl"),
    )
    depth, row, col = ("y", "core"), ("x", "zh"), "zl"
    return jax.shard_map(
        on_device,
        mesh=fine,
        in_specs=(
            P(depth, row),
            P(depth, row),
            P(depth, None),
            P(row, col),
            P(row, col),
            P(row, col),
            P(row, col),
            P(depth + row, col),
        ),
        out_specs=(
            P(depth + (col,), row),
            P(row, (col,) + depth),
            P(row, (col,) + depth),
        ),
        check_vma=False,
    )
```
